512 devices in a mesh: group: 8 (over z_lo), fsdp: 64 (over y, z_hi, x, core).
Axes of the slice: x: 4, y: 4, z: 16 (z_hi: 2, z_lo: 8; z = z_hi * 8 + z_lo), core: 2. Of those that a mesh axis runs over, the one named last changes fastest.
Arguments:
- outer_params: float32 [256, 28672], P('fsdp'), may hold values from -6 to 6
- outer_momentum: float32 [256, 28672], P('fsdp'), may hold values from -4 to 4
- first_moment: float32 [8, 256, 28672], P('group', 'fsdp'), may hold values from -0.0029296875 to 0.0029296875
- second_moment: float32 [8, 256, 28672], P('group', 'fsdp'), may hold values from 2.7247838e-08 to 2.724784e-07
- inner_grads: bfloat16 [8, 4, 256, 28672], P('group', None, 'fsdp'), may hold values from -120 to 120
Outputs:
- new_params: float32 [256, 28672], P('fsdp')
- new_momentum: float32 [256, 28672], P('fsdp')
The draws below stay inside these ranges and needn't reach their ends.
All inputs are finite; a program needn't handle non-finite values.
Results may differ from the reference program's by a relative error of at most 0.0034.
Values may be sent and summed in bfloat16 or wider, within the bound.
No kernel may reach another device: no remote copies, remote signals or barrier semaphores. Data moves between devices by JAX's collectives and lax.ppermute only.
A program may use at most 64 MiB of HBM per device.

```python
import math
import jax
import jax.numpy as jnp
from jax import lax

FF = 28672
ROW_DEV = 4
STEPS = 4
ROWS = 256
REPLICAS = 8


def draw_inner_grads(key, part):
    key = jax.random.fold_in(key, 11)
    keys = jax.random.split(key, 8)
    shape = (REPLICAS, STEPS, ROWS, FF)
    shards = ROWS // ROW_DEV
    loudest = 48.0
    base_scale = 120.0 / (4.0 * 3.0 * 10.0 * 10.0 * loudest)
    row_pos = lax.broadcasted_iota(jnp.float32, (1, 1, ROWS, 1), 2)
    ramp = 1.0 + 2.0 * row_pos / max(ROWS - 1, 1)
    row_scale = jnp.exp(math.log(10.0) * jax.random.uniform(keys[0], (REPLICAS, STEPS, ROWS, 1)))
    col_scale = jnp.exp(math.log(10.0) * jax.random.uniform(keys[1], (REPLICAS, STEPS, 1, FF)))
    base = jnp.clip(jax.random.normal(keys[3], shape), -4.0, 4.0)
    shard_level = jnp.exp(0.5 * math.log(10.0) * jax.random.uniform(keys[5], (REPLICAS, STEPS, shards, 1)))
    loud_shard = jax.random.randint(keys[6], (REPLICAS, STEPS, 1, 1), 0, shards)
    shard_pos = lax.broadcasted_iota(jnp.int32, (1, 1, shards, 1), 2)
    shard_level = jnp.where(shard_pos == loud_shard, loudest, shard_level)
    row_level = jnp.repeat(shard_level, ROW_DEV, axis=2)
    step_level = jnp.exp(-1.5 * math.log(10.0) * jax.random.uniform(keys[7], (REPLICAS, STEPS, 1, 1)))
    power_bound = (3.9 * (shards - 1) + loudest * loudest * 2.08) / shards
    quiet = 0.15 / math.sqrt(base_scale * base_scale * 2002.0 * ROWS * FF * power_bound)
    quiet_step = jax.random.randint(keys[4], (REPLICAS, 1, 1, 1), 0, STEPS)
    step_pos = lax.broadcasted_iota(jnp.int32, (1, STEPS, 1, 1), 1)
    level = jnp.where(step_pos == quiet_step, quiet, step_level)
    values = base_scale * base * ramp * row_scale * col_scale * row_level * level
    return values.astype(jnp.bfloat16)


def shard_levels(key, shape, cuts, least, high):
    def one(dim, shards_of):
        draws = jax.random.uniform(jax.random.fold_in(jax.random.fold_in(key, 6), dim), (shards_of,), jnp.float32, least / len(cuts), high / len(cuts))
        return jnp.repeat(jnp.exp(draws), shape[dim] // shards_of).reshape((-1,) + (1,) * (len(shape) - dim - 1))

    level = one(*cuts[0])
    for cut in cuts[1:]:
        level = level * one(*cut)
    return level


def centred(stream_key, extent, spread, bound, cuts=(), kind=jnp.bfloat16):
    array = jax.random.normal(stream_key, extent, jnp.float32) * spread
    if len(cuts) > 0:
        array = shard_levels(stream_key, extent, cuts, -0.22, 0.18) * array
    return jnp.clip(array, min=-bound, max=bound).astype(kind)


def setup_inputs(seed: int = 0) -> dict:
    arg_keys = jax.random.split(jax.random.key(seed), 6)
    return {
        "outer_params": centred(arg_keys[0], (ROWS, FF), 1.0, 6.0, ((0, 64),), jnp.float32),
        "outer_momentum": centred(arg_keys[1], (ROWS, FF), 0.3, 4.0, ((0, 64),), jnp.float32),
        "first_moment": centred(arg_keys[2], (REPLICAS, ROWS, FF), (0.5 / (ROWS * FF) ** 0.5), 0.0029296875, ((0, 8), (1, 64)), jnp.float32),
        "second_moment": jnp.clip(jnp.exp(math.log(2.7247838829680404e-07) - 2.3025851 * jax.random.uniform(arg_keys[3], (REPLICAS, ROWS, FF), jnp.float32) ** shard_levels(arg_keys[3], (REPLICAS, ROWS, FF), ((0, 8), (1, 64)), -0.2, 0.2)), 2.72478377638663e-08, 2.7247838829680404e-07),
        "inner_grads": draw_inner_grads(jax.random.fold_in(arg_keys[5], 71), 0),
    }


clip_norm = 1.0
beta_one = 0.9
beta_two = 0.95
inner_rate = 0.05
decay_rate = 0.1
epsilon = 1e-08
code_range = 448.0
outer_beta = 0.9
outer_rate = 0.7

def adam_steps(start, grads, moment_one, moment_two):
    params = start
    for step in range(STEPS):
        grad = grads[step].astype(jnp.float32)
        total = jnp.sum(grad * grad)
        factor = jnp.minimum(1.0, clip_norm / (jnp.sqrt(total) + 1e-06))
        grad = grad * factor
        moment_one = beta_one * moment_one + (1.0 - beta_one) * grad
        moment_two = beta_two * moment_two + (1.0 - beta_two) * grad * grad
        params = params - inner_rate * (moment_one / (jnp.sqrt(moment_two) + epsilon) + decay_rate * params)
    return params

def encode(delta):
    blocks = delta.reshape(ROWS, FF // 128, 128)
    largest = lax.optimization_barrier(jnp.max(jnp.abs(blocks), axis=-1))
    scales = (largest + 1e-06) / code_range
    codes = (blocks / scales[..., None]).astype(jnp.bfloat16)
    return (codes, scales)

def reference(outer_params, outer_momentum, first_moment, second_moment, inner_grads):
    total_delta = jnp.zeros((ROWS, FF), jnp.float32)
    for group in range(REPLICAS):
        inner = adam_steps(outer_params, inner_grads[group], first_moment[group], second_moment[group])
        codes, scales = encode(outer_params - inner)
        decoded = (codes.astype(jnp.float32) * scales[..., None]).reshape(ROWS, FF)
        total_delta = total_delta + decoded
    average = total_delta / REPLICAS
    new_momentum = outer_beta * outer_momentum + average
    new_params = outer_params - outer_rate * (average + outer_beta * new_momentum)
    return (new_params, new_momentum)
```

```python
import jax
import jax.numpy as jnp
from jax import lax
from jax.experimental import pallas as pl
from jax.experimental.pallas import tpu as pltpu
from jax.sharding import PartitionSpec as P

clip_norm = 1.0
beta_one = 0.9
beta_two = 0.95
inner_rate = 0.05
decay_rate = 0.1
epsilon = 1e-08
outer_beta = 0.9
outer_rate = 0.7
sent = jnp.bfloat16


def to_rows(x):
    lead = x.shape[:-2]
    rows, width = x.shape[-2:]
    x = x.reshape(lead + (rows, width // 128, 128))
    x = jnp.swapaxes(x, -3, -2)
    return x.reshape(lead + (rows * width // 128, 128))


def from_rows(x, rows, width):
    return jnp.swapaxes(x.reshape(width // 128, rows, 128), 0, 1).reshape(rows, width)


def squares_kernel(grads_ref, out_ref):
    steps, length, _ = grads_ref.shape
    lane = lax.broadcasted_iota(jnp.int32, (1, 128), 1)
    row = jnp.zeros((1, 128), jnp.float32)
    for step in range(steps):
        total = jnp.zeros((16, 128), jnp.float32)
        for at in range(0, length, 16):
            grad = grads_ref[step, at : at + 16, :].astype(jnp.float32)
            total = total + grad * grad
        row = jnp.where(lane == step, jnp.sum(total), row)
    out_ref[...] = jnp.broadcast_to(row, out_ref.shape)


def inner_kernel(totals_ref, params_ref, one_ref, two_ref, grads_ref, out_ref):
    steps, length, _ = grads_ref.shape
    totals = jnp.sum(totals_ref[...], axis=0, keepdims=True)
    factors = jnp.minimum(1.0, clip_norm / (jnp.sqrt(totals) + 1e-06))
    lane = lax.broadcasted_iota(jnp.int32, (1, 128), 1)
    factor = [jnp.sum(jnp.where(lane == step, factors, 0.0)) for step in range(steps)]
    for at in range(0, length, 16):
        rows = slice(at, at + 16)
        start = params_ref[rows, :]
        params = start
        moment_one = one_ref[rows, :]
        moment_two = two_ref[rows, :]
        for step in range(steps):
            grad = grads_ref[step, rows, :].astype(jnp.float32) * factor[step]
            moment_one = beta_one * moment_one + (1.0 - beta_one) * grad
            moment_two = beta_two * moment_two + (1.0 - beta_two) * grad * grad
            params = params - inner_rate * (
                moment_one / (jnp.sqrt(moment_two) + epsilon) + decay_rate * params
            )
        out_ref[rows, :] = (start - params).astype(out_ref.dtype)


def mean_kernel(in_ref, out_ref):
    replicas, length, _ = in_ref.shape
    for at in range(0, length, 16):
        rows = slice(at, at + 16)
        total = in_ref[0, rows, :].astype(jnp.float32)
        for group in range(1, replicas):
            total = total + in_ref[group, rows, :].astype(jnp.float32)
        total = (total / replicas).astype(out_ref.dtype)
        for group in range(replicas):
            out_ref[group, rows, :] = total


def outer_kernel(average_ref, params_ref, momentum_ref, new_params_ref, new_momentum_ref):
    length = average_ref.shape[0]
    for at in range(0, length, 16):
        rows = slice(at, at + 16)
        average = average_ref[rows, :].astype(jnp.float32)
        momentum = outer_beta * momentum_ref[rows, :] + average
        new_momentum_ref[rows, :] = momentum
        new_params_ref[rows, :] = params_ref[rows, :] - outer_rate * (
            average + outer_beta * momentum
        )


def call(kernel, out_shape, *args):
    return pl.pallas_call(
        kernel,
        out_shape=out_shape,
        compiler_params=pltpu.CompilerParams(vmem_limit_bytes=16 * 1024 * 1024),
    )(*args)


def body(outer_params, outer_momentum, first_moment, second_moment, inner_grads):
    replicas = lax.axis_size("group")
    shards = lax.axis_size("fsdp")
    rows, width = outer_params.shape
    length = rows * width // 128
    params = to_rows(outer_params)
    momentum = to_rows(outer_momentum)
    moment_one = to_rows(first_moment[0])
    moment_two = to_rows(second_moment[0])
    grads = to_rows(inner_grads[0])
    f32 = jnp.float32
    squares = call(squares_kernel, jax.ShapeDtypeStruct((shards, 128), f32), grads)
    totals = lax.all_to_all(squares, "fsdp", 0, 0, tiled=True)
    delta = call(
        inner_kernel,
        jax.ShapeDtypeStruct((length, 128), sent),
        totals,
        params,
        moment_one,
        moment_two,
        grads,
    )
    delta = delta.reshape(replicas, length // replicas, 128)
    parts = lax.all_to_all(delta, "group", 0, 0, tiled=True)
    mean = call(mean_kernel, jax.ShapeDtypeStruct(parts.shape, sent), parts)
    average = lax.all_to_all(mean, "group", 0, 0, tiled=True).reshape(length, 128)
    out = jax.ShapeDtypeStruct((length, 128), f32)
    new_params, new_momentum = call(outer_kernel, (out, out), average, params, momentum)
    return (from_rows(new_params, rows, width), from_rows(new_momentum, rows, width))


def solution(mesh):
    return jax.shard_map(
        body,
        mesh=mesh,
        in_specs=(
            P("fsdp", None),
            P("fsdp", None),
            P("group", "fsdp", None),
            P("group", "fsdp", None),
            P("group", None, "fsdp", None),
        ),
        out_specs=(P("fsdp", None), P("fsdp", None)),
        check_vma=False,
    )
```

```python
import jax
import jax.numpy as jnp
from jax import lax
from jax.experimental import pallas as pl
from jax.experimental.pallas import tpu as pltpu
from jax.sharding import PartitionSpec as P

clip_norm = 1.0
beta_one = 0.9
beta_two = 0.95
inner_rate = 0.05
decay_rate = 0.1
epsilon = 1e-08
outer_beta = 0.9
outer_rate = 0.7
sent = jnp.bfloat16

line_order = [4, 5, 6, 7, 3, 2, 1, 0]
totals_first = ((2 * 2 + 1) * 4 + 2) * 2
totals_order = [totals_first] + [k for k in range(64) if k != totals_first]


def to_rows(x):
    lead = x.shape[:-2]
    rows, width = x.shape[-2:]
    x = x.reshape(lead + (rows, width // 128, 128))
    x = jnp.swapaxes(x, -3, -2)
    return x.reshape(lead + (rows * width // 128, 128))


def from_rows(x, rows, width):
    return jnp.swapaxes(x.reshape(width // 128, rows, 128), 0, 1).reshape(rows, width)


def squares_kernel(grads_ref, out_ref):
    steps, length, _ = grads_ref.shape
    lane = lax.broadcasted_iota(jnp.int32, (1, 128), 1)
    row = jnp.zeros((1, 128), jnp.float32)
    for step in range(steps):
        total = jnp.zeros((16, 128), jnp.float32)
        for at in range(0, length, 16):
            grad = grads_ref[step, at : at + 16, :].astype(jnp.float32)
            total = total + grad * grad
        row = jnp.where(lane == step, jnp.sum(total), row)
    out_ref[...] = jnp.broadcast_to(row, out_ref.shape)


def inner_kernel(totals_ref, params_ref, one_ref, two_ref, grads_ref, out_ref):
    steps, length, _ = grads_ref.shape
    totals = jnp.sum(totals_ref[...], axis=0, keepdims=True)
    factors = jnp.minimum(1.0, clip_norm / (jnp.sqrt(totals) + 1e-06))
    lane = lax.broadcasted_iota(jnp.int32, (1, 128), 1)
    factor = [jnp.sum(jnp.where(lane == step, factors, 0.0)) for step in range(steps)]
    for at in range(0, length, 16):
        rows = slice(at, at + 16)
        start = params_ref[rows, :]
        params = start
        moment_one = one_ref[rows, :]
        moment_two = two_ref[rows, :]
        for step in range(steps):
            grad = grads_ref[step, rows, :].astype(jnp.float32) * factor[step]
            moment_one = beta_one * moment_one + (1.0 - beta_one) * grad
            moment_two = beta_two * moment_two + (1.0 - beta_two) * grad * grad
            params = params - inner_rate * (
                moment_one / (jnp.sqrt(moment_two) + epsilon) + decay_rate * params
            )
        out_ref[rows, :] = (start - params).astype(out_ref.dtype)


def mean_kernel(in_ref, out_ref):
    replicas, length, _ = in_ref.shape
    for at in range(0, length, 16):
        rows = slice(at, at + 16)
        total = in_ref[0, rows, :].astype(jnp.float32)
        for group in range(1, replicas):
            total = total + in_ref[group, rows, :].astype(jnp.float32)
        total = (total / replicas).astype(out_ref.dtype)
        for group in range(replicas):
            out_ref[group, rows, :] = total


def outer_kernel(average_ref, params_ref, momentum_ref, new_params_ref, new_momentum_ref):
    length = average_ref.shape[0]
    for at in range(0, length, 16):
        rows = slice(at, at + 16)
        average = average_ref[rows, :].astype(jnp.float32)
        momentum = outer_beta * momentum_ref[rows, :] + average
        new_momentum_ref[rows, :] = momentum
        new_params_ref[rows, :] = params_ref[rows, :] - outer_rate * (
            average + outer_beta * momentum
        )


def call(kernel, out_shape, *args):
    return pl.pallas_call(
        kernel,
        out_shape=out_shape,
        compiler_params=pltpu.CompilerParams(vmem_limit_bytes=16 * 1024 * 1024),
    )(*args)


def body(outer_params, outer_momentum, first_moment, second_moment, inner_grads):
    replicas = lax.axis_size("group")
    shards = lax.axis_size("fsdp")
    rows, width = outer_params.shape
    length = rows * width // 128
    params = to_rows(outer_params)
    momentum = to_rows(outer_momentum)
    moment_one = to_rows(first_moment[0])
    moment_two = to_rows(second_moment[0])
    grads = to_rows(inner_grads[0])
    f32 = jnp.float32
    squares = call(squares_kernel, jax.ShapeDtypeStruct((shards, 128), f32), grads)
    totals = lax.all_to_all(squares, "fsdp", 0, 0, tiled=True, axis_index_groups=[totals_order])
    delta = call(
        inner_kernel,
        jax.ShapeDtypeStruct((length, 128), sent),
        totals,
        params,
        moment_one,
        moment_two,
        grads,
    )
    delta = delta.reshape(replicas, length // replicas, 128)
    parts = lax.all_to_all(delta, "group", 0, 0, tiled=True, axis_index_groups=[line_order])
    mean = call(mean_kernel, jax.ShapeDtypeStruct(parts.shape, sent), parts)
    average = lax.all_to_all(mean, "group", 0, 0, tiled=True, axis_index_groups=[line_order])
    average = average.reshape(length, 128)
    out = jax.ShapeDtypeStruct((length, 128), f32)
    new_params, new_momentum = call(outer_kernel, (out, out), average, params, momentum)
    return (from_rows(new_params, rows, width), from_rows(new_momentum, rows, width))


def solution(mesh):
    return jax.shard_map(
        body,
        mesh=mesh,
        in_specs=(
            P("fsdp", None),
            P("fsdp", None),
            P("group", "fsdp", None),
            P("group", "fsdp", None),
            P("group", None, "fsdp", None),
        ),
        out_specs=(P("fsdp", None), P("fsdp", None)),
        check_vma=False,
    )
```

```python
import jax
import jax.numpy as jnp
from jax import lax
from jax.experimental import pallas as pl
from jax.experimental.pallas import tpu as pltpu
from jax.sharding import PartitionSpec as P

clip_norm = 1.0
beta_one = 0.9
beta_two = 0.95
inner_rate = 0.05
decay_rate = 0.1
epsilon = 1e-08
outer_beta = 0.9
outer_rate = 0.7
sent = jnp.bfloat16

codes_order = [4, 6, 7, 0, 1, 5, 3, 2]
means_order = [4, 6, 1, 2, 5, 3, 0, 7]
totals_first = ((2 * 2 + 1) * 4 + 2) * 2
totals_order = [totals_first] + [k for k in range(64) if k != totals_first]


def to_rows(x):
    lead = x.shape[:-2]
    rows, width = x.shape[-2:]
    x = x.reshape(lead + (rows, width // 128, 128))
    x = jnp.swapaxes(x, -3, -2)
    return x.reshape(lead + (rows * width // 128, 128))


def from_rows(x, rows, width):
    return jnp.swapaxes(x.reshape(width // 128, rows, 128), 0, 1).reshape(rows, width)


def squares_kernel(*refs):
    grads_refs, out_ref = refs[:-1], refs[-1]
    steps, (length, _) = len(grads_refs), grads_refs[0].shape
    lane = lax.broadcasted_iota(jnp.int32, (1, 128), 1)
    row = jnp.zeros((1, 128), jnp.float32)
    for step in range(steps):
        total = jnp.zeros((16, 128), jnp.float32)
        for at in range(0, length, 16):
            grad = grads_refs[step][at : at + 16, :].astype(jnp.float32)
            total = total + grad * grad
        row = jnp.where(lane == step, jnp.sum(total), row)
    out_ref[...] = jnp.broadcast_to(row, out_ref.shape)


def inner_kernel(totals_ref, params_ref, one_ref, two_ref, *refs):
    grads_refs, out_ref = refs[:-1], refs[-1]
    steps, (length, _) = len(grads_refs), grads_refs[0].shape
    totals = jnp.sum(totals_ref[...], axis=0, keepdims=True)
    factors = jnp.minimum(1.0, clip_norm / (jnp.sqrt(totals) + 1e-06))
    lane = lax.broadcasted_iota(jnp.int32, (1, 128), 1)
    kept = (1.0 - inner_rate * decay_rate) ** steps
    adds_one, adds_two, terms, weights = [], [], [], []
    for step in range(steps):
        factor = jnp.sum(jnp.where(lane == step, factors, 0.0))
        shrunk_one = beta_one ** (step + 1)
        shrunk_two = beta_two ** (step + 1)
        left = (1.0 - inner_rate * decay_rate) ** (steps - 1 - step)
        adds_one.append(factor * ((1.0 - beta_one) / shrunk_one))
        adds_two.append(factor * factor * ((1.0 - beta_two) / shrunk_two))
        terms.append(epsilon / shrunk_two**0.5)
        weights.append(inner_rate * left * shrunk_one / shrunk_two**0.5)
    for at in range(0, length, 16):
        rows = slice(at, at + 16)
        delta = (1.0 - kept) * params_ref[rows, :]
        moment_one = one_ref[rows, :]
        moment_two = two_ref[rows, :]
        for step in range(steps):
            grad = grads_refs[step][rows, :].astype(jnp.float32)
            moment_one = moment_one + adds_one[step] * grad
            moment_two = moment_two + adds_two[step] * (grad * grad)
            root = moment_two * lax.rsqrt(moment_two) + terms[step]
            delta = delta + (weights[step] * moment_one) / root
        out_ref[rows, :] = delta.astype(out_ref.dtype)


def mean_kernel(in_ref, out_ref):
    replicas, length, _ = in_ref.shape
    for at in range(0, length, 16):
        rows = slice(at, at + 16)
        total = in_ref[0, rows, :].astype(jnp.float32)
        for group in range(1, replicas):
            total = total + in_ref[group, rows, :].astype(jnp.float32)
        total = (total / replicas).astype(out_ref.dtype)
        for group in range(replicas):
            out_ref[group, rows, :] = total


def outer_kernel(average_ref, params_ref, momentum_ref, new_params_ref, new_momentum_ref):
    _, length, _ = average_ref.shape
    for part, owner in enumerate(codes_order):
        slot = means_order.index(owner)
        for at in range(0, length, 16):
            rows = slice(part * length + at, part * length + at + 16)
            average = average_ref[slot, at : at + 16, :].astype(jnp.float32)
            momentum = outer_beta * momentum_ref[rows, :] + average
            new_momentum_ref[rows, :] = momentum
            new_params_ref[rows, :] = params_ref[rows, :] - outer_rate * (
                average + outer_beta * momentum
            )


def call(kernel, out_shape, *args):
    return pl.pallas_call(
        kernel,
        out_shape=out_shape,
        compiler_params=pltpu.CompilerParams(vmem_limit_bytes=16 * 1024 * 1024),
    )(*args)


def body(outer_params, outer_momentum, first_moment, second_moment, inner_grads):
    replicas = lax.axis_size("group")
    shards = lax.axis_size("fsdp")
    rows, width = outer_params.shape
    length = rows * width // 128
    params = to_rows(outer_params)
    momentum = to_rows(outer_momentum)
    moment_one = to_rows(first_moment[0])
    moment_two = to_rows(second_moment[0])
    grads = [to_rows(inner_grads[0, step]) for step in range(inner_grads.shape[1])]
    f32 = jnp.float32
    squares = call(squares_kernel, jax.ShapeDtypeStruct((shards, 128), f32), *grads)
    totals = lax.all_to_all(squares, "fsdp", 0, 0, tiled=True, axis_index_groups=[totals_order])
    delta = call(
        inner_kernel,
        jax.ShapeDtypeStruct((length, 128), sent),
        totals,
        params,
        moment_one,
        moment_two,
        *grads,
    )
    delta = delta.reshape(replicas, length // replicas, 128)
    parts = lax.all_to_all(delta, "group", 0, 0, tiled=True, axis_index_groups=[codes_order])
    mean = call(mean_kernel, jax.ShapeDtypeStruct(parts.shape, sent), parts)
    average = lax.all_to_all(mean, "group", 0, 0, tiled=True, axis_index_groups=[means_order])
    out = jax.ShapeDtypeStruct((length, 128), f32)
    new_params, new_momentum = call(outer_kernel, (out, out), average, params, momentum)
    return (from_rows(new_params, rows, width), from_rows(new_momentum, rows, width))


def solution(mesh):
    return jax.shard_map(
        body,
        mesh=mesh,
        in_specs=(
            P("fsdp", None),
            P("fsdp", None),
            P("group", "fsdp", None),
            P("group", "fsdp", None),
            P("group", None, "fsdp", None),
        ),
        out_specs=(P("fsdp", None), P("fsdp", None)),
        check_vma=False,
    )
```

```python
import jax
import jax.numpy as jnp
from jax import lax
from jax.experimental import pallas as pl
from jax.experimental.pallas import tpu as pltpu
from jax.sharding import PartitionSpec as P

clip_norm = 1.0
beta_one = 0.9
beta_two = 0.95
inner_rate = 0.05
decay_rate = 0.1
epsilon = 1e-08
outer_beta = 0.9
outer_rate = 0.7
sent = jnp.bfloat16

codes_order = [4, 6, 7, 0, 1, 5, 3, 2]
means_order = [4, 2, 1, 7, 5, 3, 0, 6]
totals_first = ((2 * 2 + 1) * 4 + 2) * 2
totals_order = [totals_first] + [k for k in range(64) if k != totals_first]


def to_rows(x):
    lead = x.shape[:-2]
    rows, width = x.shape[-2:]
    x = x.reshape(lead + (rows, width // 128, 128))
    x = jnp.swapaxes(x, -3, -2)
    return x.reshape(lead + (rows * width // 128, 128))


def from_rows(x, rows, width):
    return jnp.swapaxes(x.reshape(width // 128, rows, 128), 0, 1).reshape(rows, width)


def squares_kernel(*refs):
    grads_refs, out_ref = refs[:-1], refs[-1]
    steps, (length, _) = len(grads_refs), grads_refs[0].shape
    lane = lax.broadcasted_iota(jnp.int32, (1, 128), 1)
    row = jnp.zeros((1, 128), jnp.float32)
    for step in range(steps):
        total = jnp.zeros((16, 128), jnp.float32)
        for at in range(0, length, 16):
            grad = grads_refs[step][at : at + 16, :].astype(jnp.float32)
            total = total + grad * grad
        row = jnp.where(lane == step, jnp.sum(total), row)
    out_ref[...] = jnp.broadcast_to(row, out_ref.shape)


def inner_kernel(totals_ref, params_ref, one_ref, two_ref, *refs):
    grads_refs, out_ref = refs[:-1], refs[-1]
    steps, (length, _) = len(grads_refs), grads_refs[0].shape
    totals = jnp.sum(totals_ref[...], axis=0, keepdims=True)
    factors = jnp.minimum(1.0, clip_norm / (jnp.sqrt(totals) + 1e-06))
    lane = lax.broadcasted_iota(jnp.int32, (1, 128), 1)
    kept = (1.0 - inner_rate * decay_rate) ** steps
    adds_one, adds_two, terms, weights = [], [], [], []
    for step in range(steps):
        factor = jnp.sum(jnp.where(lane == step, factors, 0.0))
        shrunk_one = beta_one ** (step + 1)
        shrunk_two = beta_two ** (step + 1)
        left = (1.0 - inner_rate * decay_rate) ** (steps - 1 - step)
        adds_one.append(factor * ((1.0 - beta_one) / shrunk_one))
        adds_two.append(factor * factor * ((1.0 - beta_two) / shrunk_two))
        terms.append(epsilon / shrunk_two**0.5)
        weights.append(inner_rate * left * shrunk_one / shrunk_two**0.5)
    for at in range(0, length, 16):
        rows = slice(at, at + 16)
        delta = (1.0 - kept) * params_ref[rows, :]
        moment_one = one_ref[rows, :]
        moment_two = two_ref[rows, :]
        for step in range(steps):
            grad = grads_refs[step][rows, :].astype(jnp.float32)
            moment_one = moment_one + adds_one[step] * grad
            moment_two = moment_two + adds_two[step] * (grad * grad)
            root = moment_two * lax.rsqrt(moment_two) + terms[step]
            delta = delta + (weights[step] * moment_one) / root
        out_ref[rows, :] = delta.astype(out_ref.dtype)


def mean_kernel(in_ref, out_ref):
    replicas, length, _ = in_ref.shape
    for at in range(0, length, 16):
        rows = slice(at, at + 16)
        total = in_ref[0, rows, :].astype(jnp.float32)
        for group in range(1, replicas):
            total = total + in_ref[group, rows, :].astype(jnp.float32)
        total = (total / replicas).astype(out_ref.dtype)
        for group in range(replicas):
            out_ref[group, rows, :] = total


def outer_kernel(average_ref, params_ref, momentum_ref, new_params_ref, new_momentum_ref):
    _, length, _ = average_ref.shape
    for part, owner in enumerate(codes_order):
        slot = means_order.index(owner)
        for at in range(0, length, 16):
            rows = slice(part * length + at, part * length + at + 16)
            average = average_ref[slot, at : at + 16, :].astype(jnp.float32)
            momentum = outer_beta * momentum_ref[rows, :] + average
            new_momentum_ref[rows, :] = momentum
            new_params_ref[rows, :] = params_ref[rows, :] - outer_rate * (
                average + outer_beta * momentum
            )


def call(kernel, out_shape, *args):
    return pl.pallas_call(
        kernel,
        out_shape=out_shape,
        compiler_params=pltpu.CompilerParams(vmem_limit_bytes=16 * 1024 * 1024),
    )(*args)


def body(outer_params, outer_momentum, first_moment, second_moment, inner_grads):
    replicas = lax.axis_size("group")
    shards = lax.axis_size("fsdp")
    rows, width = outer_params.shape
    length = rows * width // 128
    params = to_rows(outer_params)
    momentum = to_rows(outer_momentum)
    moment_one = to_rows(first_moment[0])
    moment_two = to_rows(second_moment[0])
    grads = [to_rows(inner_grads[0, step]) for step in range(inner_grads.shape[1])]
    f32 = jnp.float32
    squares = call(squares_kernel, jax.ShapeDtypeStruct((shards, 128), f32), *grads)
    totals = lax.all_to_all(squares, "fsdp", 0, 0, tiled=True, axis_index_groups=[totals_order])
    delta = call(
        inner_kernel,
        jax.ShapeDtypeStruct((length, 128), sent),
        totals,
        params,
        moment_one,
        moment_two,
        *grads,
    )
    delta = delta.reshape(replicas, length // replicas, 128)
    parts = lax.all_to_all(delta, "group", 0, 0, tiled=True, axis_index_groups=[codes_order])
    mean = call(mean_kernel, jax.ShapeDtypeStruct(parts.shape, sent), parts)
    average = lax.all_to_all(mean, "group", 0, 0, tiled=True, axis_index_groups=[means_order])
    out = jax.ShapeDtypeStruct((length, 128), f32)
    new_params, new_momentum = call(outer_kernel, (out, out), average, params, momentum)
    return (from_rows(new_params, rows, width), from_rows(new_momentum, rows, width))


def solution(mesh):
    return jax.shard_map(
        body,
        mesh=mesh,
        in_specs=(
            P("fsdp", None),
            P("fsdp", None),
            P("group", "fsdp", None),
            P("group", "fsdp", None),
            P("group", None, "fsdp", None),
        ),
        out_specs=(P("fsdp", None), P("fsdp", None)),
        check_vma=False,
    )
```

```python
import jax
import jax.numpy as jnp
from jax import lax
from jax.experimental import pallas as pl
from jax.experimental.pallas import tpu as pltpu
from jax.sharding import PartitionSpec as P

clip_norm = 1.0
beta_one = 0.9
beta_two = 0.95
inner_rate = 0.05
decay_rate = 0.1
epsilon = 1e-08
outer_beta = 0.9
outer_rate = 0.7
sent = jnp.bfloat16

codes_order = [4, 6, 7, 0, 1, 5, 3, 2]
means_order = [4, 2, 1, 7, 5, 3, 0, 6]
totals_first = ((2 * 2 + 1) * 4 + 2) * 2
totals_order = [totals_first] + [k for k in range(64) if k != totals_first]


def to_rows(x):
    lead = x.shape[:-2]
    rows, width = x.shape[-2:]
    x = x.reshape(lead + (rows, width // 128, 128))
    x = jnp.swapaxes(x, -3, -2)
    return x.reshape(lead + (rows * width // 128, 128))


def in_hbm(x):
    return pltpu.with_memory_space_constraint(x, pltpu.HBM)


def from_rows(x, rows, width):
    return jnp.swapaxes(x.reshape(width // 128, rows, 128), 0, 1).reshape(rows, width)


def squares_kernel(grads_ref, two_ref, out_ref, grads_held_ref, two_held_ref, sems, two_sem):
    steps, length, _ = grads_ref.shape
    copies = [
        pltpu.make_async_copy(grads_ref.at[step], grads_held_ref.at[step], sems.at[step])
        for step in range(steps)
    ]
    two_copy = pltpu.make_async_copy(two_ref, two_held_ref, two_sem)
    for copy in copies:
        copy.start()
    two_copy.start()
    lane = lax.broadcasted_iota(jnp.int32, (1, 128), 1)
    row = jnp.zeros((1, 128), jnp.float32)
    for step in range(steps):
        copies[step].wait()
        total = jnp.zeros((16, 128), jnp.float32)
        for at in range(0, length, 16):
            grad = grads_held_ref[step, at : at + 16, :].astype(jnp.float32)
            total = total + grad * grad
        row = jnp.where(lane == step, jnp.sum(total), row)
    out_ref[...] = jnp.broadcast_to(row, out_ref.shape)
    two_copy.wait()


def inner_kernel(totals_ref, params_ref, one_ref, two_ref, grads_ref, out_ref):
    steps, length, _ = grads_ref.shape
    totals = jnp.sum(totals_ref[...], axis=0, keepdims=True)
    factors = jnp.minimum(1.0, clip_norm / (jnp.sqrt(totals) + 1e-06))
    lane = lax.broadcasted_iota(jnp.int32, (1, 128), 1)
    kept = (1.0 - inner_rate * decay_rate) ** steps
    adds_one, adds_two, terms, weights = [], [], [], []
    for step in range(steps):
        factor = jnp.sum(jnp.where(lane == step, factors, 0.0))
        shrunk_one = beta_one ** (step + 1)
        shrunk_two = beta_two ** (step + 1)
        left = (1.0 - inner_rate * decay_rate) ** (steps - 1 - step)
        adds_one.append(factor * ((1.0 - beta_one) / shrunk_one))
        adds_two.append(factor * factor * ((1.0 - beta_two) / shrunk_two))
        terms.append(epsilon / shrunk_two**0.5)
        weights.append(inner_rate * left * shrunk_one / shrunk_two**0.5)
    for at in range(0, length, 16):
        rows = slice(at, at + 16)
        delta = (1.0 - kept) * params_ref[rows, :]
        moment_one = one_ref[rows, :]
        moment_two = two_ref[rows, :]
        for step in range(steps):
            grad = grads_ref[step, rows, :].astype(jnp.float32)
            moment_one = moment_one + adds_one[step] * grad
            moment_two = moment_two + adds_two[step] * (grad * grad)
            root = moment_two * lax.rsqrt(moment_two) + terms[step]
            delta = delta + (weights[step] * moment_one) / root
        out_ref[rows, :] = delta.astype(out_ref.dtype)


def mean_kernel(in_ref, out_ref):
    replicas, length, _ = in_ref.shape
    for at in range(0, length, 16):
        rows = slice(at, at + 16)
        total = in_ref[0, rows, :].astype(jnp.float32)
        for group in range(1, replicas):
            total = total + in_ref[group, rows, :].astype(jnp.float32)
        total = (total / replicas).astype(out_ref.dtype)
        for group in range(replicas):
            out_ref[group, rows, :] = total


def outer_kernel(average_ref, params_ref, momentum_ref, new_params_ref, new_momentum_ref):
    _, length, _ = average_ref.shape
    for part, owner in enumerate(codes_order):
        slot = means_order.index(owner)
        for at in range(0, length, 16):
            rows = slice(part * length + at, part * length + at + 16)
            average = average_ref[slot, at : at + 16, :].astype(jnp.float32)
            momentum = outer_beta * momentum_ref[rows, :] + average
            new_momentum_ref[rows, :] = momentum
            new_params_ref[rows, :] = params_ref[rows, :] - outer_rate * (
                average + outer_beta * momentum
            )


def call(kernel, out_shape, *args, space=pltpu.VMEM, scratch=()):
    return pl.pallas_call(
        kernel,
        out_shape=out_shape,
        in_specs=[pl.BlockSpec(memory_space=space)] * len(args),
        scratch_shapes=scratch,
        compiler_params=pltpu.CompilerParams(vmem_limit_bytes=16 * 1024 * 1024),
    )(*args)


def body(outer_params, outer_momentum, first_moment, second_moment, inner_grads):
    replicas = lax.axis_size("group")
    shards = lax.axis_size("fsdp")
    rows, width = outer_params.shape
    length = rows * width // 128
    params = to_rows(outer_params)
    momentum = to_rows(outer_momentum)
    moment_one = to_rows(first_moment[0])
    moment_two = in_hbm(to_rows(second_moment[0]))
    grads = in_hbm(to_rows(inner_grads[0]))
    f32 = jnp.float32
    squares, grads, moment_two = call(
        squares_kernel,
        (
            jax.ShapeDtypeStruct((shards, 128), f32),
            jax.ShapeDtypeStruct(grads.shape, grads.dtype),
            jax.ShapeDtypeStruct(moment_two.shape, moment_two.dtype),
        ),
        grads,
        moment_two,
        space=pltpu.HBM,
        scratch=(pltpu.SemaphoreType.DMA((grads.shape[0],)), pltpu.SemaphoreType.DMA),
    )
    totals = lax.all_to_all(squares, "fsdp", 0, 0, tiled=True, axis_index_groups=[totals_order])
    delta = call(
        inner_kernel,
        jax.ShapeDtypeStruct((length, 128), sent),
        totals,
        params,
        moment_one,
        moment_two,
        grads,
    )
    delta = delta.reshape(replicas, length // replicas, 128)
    parts = lax.all_to_all(delta, "group", 0, 0, tiled=True, axis_index_groups=[codes_order])
    mean = call(mean_kernel, jax.ShapeDtypeStruct(parts.shape, sent), parts)
    average = lax.all_to_all(mean, "group", 0, 0, tiled=True, axis_index_groups=[means_order])
    out = jax.ShapeDtypeStruct((length, 128), f32)
    new_params, new_momentum = call(outer_kernel, (out, out), average, params, momentum)
    return (from_rows(new_params, rows, width), from_rows(new_momentum, rows, width))


def solution(mesh):
    return jax.shard_map(
        body,
        mesh=mesh,
        in_specs=(
            P("fsdp", None),
            P("fsdp", None),
            P("group", "fsdp", None),
            P("group", "fsdp", None),
            P("group", None, "fsdp", None),
        ),
        out_specs=(P("fsdp", None), P("fsdp", None)),
        check_vma=False,
    )
```

```python
import jax
import jax.numpy as jnp
from jax import lax
from jax.experimental import pallas as pl
from jax.experimental.pallas import tpu as pltpu
from jax.sharding import PartitionSpec as P

clip_norm = 1.0
beta_one = 0.9
beta_two = 0.95
inner_rate = 0.05
decay_rate = 0.1
epsilon = 1e-08
outer_beta = 0.9
outer_rate = 0.7
sent = jnp.bfloat16

codes_order = [4, 6, 7, 0, 1, 5, 3, 2]
means_order = [4, 2, 1, 7, 5, 3, 0, 6]
totals_first = ((2 * 2 + 1) * 4 + 2) * 2 + 1
totals_order = [totals_first] + [k for k in range(64) if k != totals_first]


def to_rows(x):
    lead = x.shape[:-2]
    rows, width = x.shape[-2:]
    x = x.reshape(lead + (rows, width // 128, 128))
    x = jnp.swapaxes(x, -3, -2)
    return x.reshape(lead + (rows * width // 128, 128))


def in_hbm(x):
    return pltpu.with_memory_space_constraint(x, pltpu.HBM)


def from_rows(x, rows, width):
    return jnp.swapaxes(x.reshape(width // 128, rows, 128), 0, 1).reshape(rows, width)


def squares_kernel(grads_ref, two_ref, out_ref, grads_held_ref, two_held_ref, sems, two_sem):
    steps, length, _ = grads_ref.shape
    copies = [
        pltpu.make_async_copy(grads_ref.at[step], grads_held_ref.at[step], sems.at[step])
        for step in range(steps)
    ]
    two_copy = pltpu.make_async_copy(two_ref, two_held_ref, two_sem)
    for copy in copies:
        copy.start()
    two_copy.start()
    lane = lax.broadcasted_iota(jnp.int32, (1, 128), 1)
    row = jnp.zeros((1, 128), jnp.float32)
    for step in range(steps):
        copies[step].wait()
        total = jnp.zeros((16, 128), jnp.float32)
        for at in range(0, length, 16):
            grad = grads_held_ref[step, at : at + 16, :].astype(jnp.float32)
            total = total + grad * grad
        row = jnp.where(lane == step, jnp.sum(total), row)
    out_ref[...] = jnp.broadcast_to(row, out_ref.shape)
    two_copy.wait()


def inner_kernel(totals_ref, params_ref, one_ref, two_ref, grads_ref, out_ref):
    steps, length, _ = grads_ref.shape
    totals = jnp.sum(totals_ref[...], axis=0, keepdims=True)
    factors = jnp.minimum(1.0, clip_norm / (jnp.sqrt(totals) + 1e-06))
    lane = lax.broadcasted_iota(jnp.int32, (1, 128), 1)
    kept = (1.0 - inner_rate * decay_rate) ** steps
    adds_one, adds_two, terms, weights = [], [], [], []
    for step in range(steps):
        factor = jnp.sum(jnp.where(lane == step, factors, 0.0))
        shrunk_one = beta_one ** (step + 1)
        shrunk_two = beta_two ** (step + 1)
        left = (1.0 - inner_rate * decay_rate) ** (steps - 1 - step)
        adds_one.append(factor * ((1.0 - beta_one) / shrunk_one))
        adds_two.append(factor * factor * ((1.0 - beta_two) / shrunk_two))
        terms.append(epsilon / shrunk_two**0.5)
        weights.append(inner_rate * left * shrunk_one / shrunk_two**0.5)
    for at in range(0, length, 16):
        rows = slice(at, at + 16)
        delta = (1.0 - kept) * params_ref[rows, :]
        moment_one = one_ref[rows, :]
        moment_two = two_ref[rows, :]
        for step in range(steps):
            grad = grads_ref[step, rows, :].astype(jnp.float32)
            moment_one = moment_one + adds_one[step] * grad
            moment_two = moment_two + adds_two[step] * (grad * grad)
            root = moment_two * lax.rsqrt(moment_two) + terms[step]
            delta = delta + (weights[step] * moment_one) / root
        out_ref[rows, :] = delta.astype(out_ref.dtype)


def mean_kernel(in_ref, out_ref):
    replicas, length, _ = in_ref.shape
    for at in range(0, length, 16):
        rows = slice(at, at + 16)
        total = in_ref[0, rows, :].astype(jnp.float32)
        for group in range(1, replicas):
            total = total + in_ref[group, rows, :].astype(jnp.float32)
        total = (total / replicas).astype(out_ref.dtype)
        for group in range(replicas):
            out_ref[group, rows, :] = total


def outer_kernel(average_ref, params_ref, momentum_ref, new_params_ref, new_momentum_ref):
    _, length, _ = average_ref.shape
    for part, owner in enumerate(codes_order):
        slot = means_order.index(owner)
        for at in range(0, length, 16):
            rows = slice(part * length + at, part * length + at + 16)
            average = average_ref[slot, at : at + 16, :].astype(jnp.float32)
            momentum = outer_beta * momentum_ref[rows, :] + average
            new_momentum_ref[rows, :] = momentum
            new_params_ref[rows, :] = params_ref[rows, :] - outer_rate * (
                average + outer_beta * momentum
            )


def call(kernel, out_shape, *args, space=pltpu.VMEM, scratch=()):
    return pl.pallas_call(
        kernel,
        out_shape=out_shape,
        in_specs=[pl.BlockSpec(memory_space=space)] * len(args),
        scratch_shapes=scratch,
        compiler_params=pltpu.CompilerParams(vmem_limit_bytes=16 * 1024 * 1024),
    )(*args)


def body(outer_params, outer_momentum, first_moment, second_moment, inner_grads):
    replicas = lax.axis_size("group")
    shards = lax.axis_size("fsdp")
    rows, width = outer_params.shape
    length = rows * width // 128
    params = to_rows(outer_params)
    momentum = to_rows(outer_momentum)
    moment_one = to_rows(first_moment[0])
    moment_two = in_hbm(to_rows(second_moment[0]))
    grads = in_hbm(to_rows(inner_grads[0]))
    f32 = jnp.float32
    squares, grads, moment_two = call(
        squares_kernel,
        (
            jax.ShapeDtypeStruct((shards, 128), f32),
            jax.ShapeDtypeStruct(grads.shape, grads.dtype),
            jax.ShapeDtypeStruct(moment_two.shape, moment_two.dtype),
        ),
        grads,
        moment_two,
        space=pltpu.HBM,
        scratch=(pltpu.SemaphoreType.DMA((grads.shape[0],)), pltpu.SemaphoreType.DMA),
    )
    totals = lax.all_to_all(squares, "fsdp", 0, 0, tiled=True, axis_index_groups=[totals_order])
    delta = call(
        inner_kernel,
        jax.ShapeDtypeStruct((length, 128), sent),
        totals,
        params,
        moment_one,
        moment_two,
        grads,
    )
    delta = delta.reshape(replicas, length // replicas, 128)
    parts = lax.all_to_all(delta, "group", 0, 0, tiled=True, axis_index_groups=[codes_order])
    mean = call(mean_kernel, jax.ShapeDtypeStruct(parts.shape, sent), parts)
    average = lax.all_to_all(mean, "group", 0, 0, tiled=True, axis_index_groups=[means_order])
    out = jax.ShapeDtypeStruct((length, 128), f32)
    new_params, new_momentum = call(outer_kernel, (out, out), average, params, momentum)
    return (from_rows(new_params, rows, width), from_rows(new_momentum, rows, width))


def solution(mesh):
    return jax.shard_map(
        body,
        mesh=mesh,
        in_specs=(
            P("fsdp", None),
            P("fsdp", None),
            P("group", "fsdp", None),
            P("group", "fsdp", None),
            P("group", None, "fsdp", None),
        ),
        out_specs=(P("fsdp", None), P("fsdp", None)),
        check_vma=False,
    )
```

```python
import jax
import jax.numpy as jnp
from jax import lax
from jax.experimental import pallas as pl
from jax.experimental.pallas import tpu as pltpu
from jax.sharding import PartitionSpec as P

clip_norm = 1.0
beta_one = 0.9
beta_two = 0.95
inner_rate = 0.05
decay_rate = 0.1
epsilon = 1e-08
outer_beta = 0.9
outer_rate = 0.7
sent = jnp.bfloat16

codes_order = [4, 6, 7, 0, 1, 5, 3, 2]
means_order = [4, 2, 1, 7, 5, 3, 0, 6]
totals_first = ((2 * 2 + 1) * 4 + 2) * 2 + 1
totals_order = [totals_first] + [k for k in range(64) if k != totals_first]


def to_rows(x):
    lead = x.shape[:-2]
    rows, width = x.shape[-2:]
    x = x.reshape(lead + (rows, width // 128, 128))
    x = jnp.swapaxes(x, -3, -2)
    return x.reshape(lead + (rows * width // 128, 128))


def in_hbm(x):
    return pltpu.with_memory_space_constraint(x, pltpu.HBM)


def from_rows(x, rows, width):
    return jnp.swapaxes(x.reshape(width // 128, rows, 128), 0, 1).reshape(rows, width)


def squares_kernel(grads_ref, two_ref, out_ref, grads_held_ref, two_held_ref, sems, two_sem):
    steps, length, _ = grads_ref.shape
    copies = [
        pltpu.make_async_copy(grads_ref.at[step], grads_held_ref.at[step], sems.at[step])
        for step in range(steps)
    ]
    two_copy = pltpu.make_async_copy(two_ref, two_held_ref, two_sem)
    for copy in copies:
        copy.start()
    two_copy.start()
    lane = lax.broadcasted_iota(jnp.int32, (1, 128), 1)
    row = jnp.zeros((1, 128), jnp.float32)
    for step in range(steps):
        copies[step].wait()
        total = jnp.zeros((16, 128), jnp.float32)
        for at in range(0, length, 16):
            grad = grads_held_ref[step, at : at + 16, :].astype(jnp.float32)
            total = total + grad * grad
        total = jnp.sum(jnp.sum(total, axis=0, keepdims=True), axis=1, keepdims=True)
        row = jnp.where(lane == step, total, row)
    out_ref[...] = jnp.broadcast_to(row, out_ref.shape)
    two_copy.wait()


def inner_kernel(totals_ref, params_ref, one_ref, two_ref, grads_ref, out_ref):
    steps, length, _ = grads_ref.shape
    totals = jnp.sum(totals_ref[...], axis=0, keepdims=True)
    factors = jnp.minimum(1.0, clip_norm / (jnp.sqrt(totals) + 1e-06))
    lane = lax.broadcasted_iota(jnp.int32, (1, 128), 1)
    kept = (1.0 - inner_rate * decay_rate) ** steps
    adds_one, adds_two, terms, weights = [], [], [], []
    for step in range(steps):
        factor = jnp.sum(jnp.where(lane == step, factors, 0.0), axis=1, keepdims=True)
        factor = jnp.broadcast_to(factor, (16, 128))
        shrunk_one = beta_one ** (step + 1)
        shrunk_two = beta_two ** (step + 1)
        left = (1.0 - inner_rate * decay_rate) ** (steps - 1 - step)
        adds_one.append(factor * ((1.0 - beta_one) / shrunk_one))
        adds_two.append(factor * factor * ((1.0 - beta_two) / shrunk_two))
        terms.append(epsilon / shrunk_two**0.5)
        weights.append(inner_rate * left * shrunk_one / shrunk_two**0.5)
    for at in range(0, length, 16):
        rows = slice(at, at + 16)
        delta = (1.0 - kept) * params_ref[rows, :]
        moment_one = one_ref[rows, :]
        moment_two = two_ref[rows, :]
        for step in range(steps):
            grad = grads_ref[step, rows, :].astype(jnp.float32)
            moment_one = moment_one + adds_one[step] * grad
            moment_two = moment_two + adds_two[step] * (grad * grad)
            root = moment_two * lax.rsqrt(moment_two) + terms[step]
            delta = delta + (weights[step] * moment_one) / root
        out_ref[rows, :] = delta.astype(out_ref.dtype)


def mean_kernel(in_ref, out_ref):
    replicas, length, _ = in_ref.shape
    for at in range(0, length, 16):
        rows = slice(at, at + 16)
        total = in_ref[0, rows, :].astype(jnp.float32)
        for group in range(1, replicas):
            total = total + in_ref[group, rows, :].astype(jnp.float32)
        total = (total / replicas).astype(out_ref.dtype)
        for group in range(replicas):
            out_ref[group, rows, :] = total


def outer_kernel(average_ref, params_ref, momentum_ref, new_params_ref, new_momentum_ref):
    _, length, _ = average_ref.shape
    for part, owner in enumerate(codes_order):
        slot = means_order.index(owner)
        for at in range(0, length, 16):
            rows = slice(part * length + at, part * length + at + 16)
            average = average_ref[slot, at : at + 16, :].astype(jnp.float32)
            momentum = outer_beta * momentum_ref[rows, :] + average
            new_momentum_ref[rows, :] = momentum
            new_params_ref[rows, :] = params_ref[rows, :] - outer_rate * (
                average + outer_beta * momentum
            )


def call(kernel, out_shape, *args, space=pltpu.VMEM, scratch=()):
    return pl.pallas_call(
        kernel,
        out_shape=out_shape,
        in_specs=[pl.BlockSpec(memory_space=space)] * len(args),
        scratch_shapes=scratch,
        compiler_params=pltpu.CompilerParams(vmem_limit_bytes=16 * 1024 * 1024),
    )(*args)


def body(outer_params, outer_momentum, first_moment, second_moment, inner_grads):
    replicas = lax.axis_size("group")
    shards = lax.axis_size("fsdp")
    rows, width = outer_params.shape
    length = rows * width // 128
    params = to_rows(outer_params)
    momentum = to_rows(outer_momentum)
    moment_one = to_rows(first_moment[0])
    moment_two = in_hbm(to_rows(second_moment[0]))
    grads = in_hbm(to_rows(inner_grads[0]))
    f32 = jnp.float32
    squares, grads, moment_two = call(
        squares_kernel,
        (
            jax.ShapeDtypeStruct((shards, 128), f32),
            jax.ShapeDtypeStruct(grads.shape, grads.dtype),
            jax.ShapeDtypeStruct(moment_two.shape, moment_two.dtype),
        ),
        grads,
        moment_two,
        space=pltpu.HBM,
        scratch=(pltpu.SemaphoreType.DMA((grads.shape[0],)), pltpu.SemaphoreType.DMA),
    )
    totals = lax.all_to_all(squares, "fsdp", 0, 0, tiled=True, axis_index_groups=[totals_order])
    delta = call(
        inner_kernel,
        jax.ShapeDtypeStruct((length, 128), sent),
        totals,
        params,
        moment_one,
        moment_two,
        grads,
    )
    delta = delta.reshape(replicas, length // replicas, 128)
    parts = lax.all_to_all(delta, "group", 0, 0, tiled=True, axis_index_groups=[codes_order])
    mean = call(mean_kernel, jax.ShapeDtypeStruct(parts.shape, sent), parts)
    average = lax.all_to_all(mean, "group", 0, 0, tiled=True, axis_index_groups=[means_order])
    out = jax.ShapeDtypeStruct((length, 128), f32)
    new_params, new_momentum = call(outer_kernel, (out, out), average, params, momentum)
    return (from_rows(new_params, rows, width), from_rows(new_momentum, rows, width))


def solution(mesh):
    return jax.shard_map(
        body,
        mesh=mesh,
        in_specs=(
            P("fsdp", None),
            P("fsdp", None),
            P("group", "fsdp", None),
            P("group", "fsdp", None),
            P("group", None, "fsdp", None),
        ),
        out_specs=(P("fsdp", None), P("fsdp", None)),
        check_vma=False,
    )
```

```python
import jax
import jax.numpy as jnp
from jax import lax
from jax.experimental import pallas as pl
from jax.experimental.pallas import tpu as pltpu
from jax.sharding import PartitionSpec as P

clip_norm = 1.0
beta_one = 0.9
beta_two = 0.95
inner_rate = 0.05
decay_rate = 0.1
epsilon = 1e-08
outer_beta = 0.9
outer_rate = 0.7
sent = jnp.bfloat16

codes_order = [4, 6, 7, 0, 1, 5, 3, 2]
means_order = [4, 2, 1, 7, 5, 3, 0, 6]
totals_first = ((2 * 2 + 1) * 4 + 2) * 2 + 1
totals_order = [totals_first] + [k for k in range(64) if k != totals_first]


def to_rows(x):
    lead = x.shape[:-2]
    rows, width = x.shape[-2:]
    x = x.reshape(lead + (rows, width // 128, 128))
    x = jnp.swapaxes(x, -3, -2)
    return x.reshape(lead + (rows * width // 128, 128))


def in_hbm(x):
    return pltpu.with_memory_space_constraint(x, pltpu.HBM)


def from_rows(x, rows, width):
    return jnp.swapaxes(x.reshape(width // 128, rows, 128), 0, 1).reshape(rows, width)


def squares_kernel(grads_ref, two_ref, out_ref, grads_held_ref, two_held_ref, sems, two_sem):
    steps, length, _ = grads_ref.shape
    copies = [
        pltpu.make_async_copy(grads_ref.at[step], grads_held_ref.at[step], sems.at[step])
        for step in range(steps)
    ]
    two_copy = pltpu.make_async_copy(two_ref, two_held_ref, two_sem)
    for copy in copies:
        copy.start()
    two_copy.start()
    lane = lax.broadcasted_iota(jnp.int32, (1, 128), 1)
    row = jnp.zeros((1, 128), jnp.float32)
    for step in range(steps):
        copies[step].wait()
        total = jnp.zeros((16, 128), jnp.float32)
        for at in range(0, length, 16):
            grad = grads_held_ref[step, at : at + 16, :].astype(jnp.float32)
            total = total + grad * grad
        total = jnp.sum(jnp.sum(total, axis=0, keepdims=True), axis=1, keepdims=True)
        row = jnp.where(lane == step, total, row)
    out_ref[...] = jnp.broadcast_to(row, out_ref.shape)
    two_copy.wait()


def inner_kernel(totals_ref, params_ref, one_ref, two_ref, grads_ref, out_ref):
    steps, length, _ = grads_ref.shape
    totals = jnp.sum(totals_ref[...], axis=0, keepdims=True)
    factors = jnp.minimum(1.0, clip_norm / (jnp.sqrt(totals) + 1e-06))
    lane = lax.broadcasted_iota(jnp.int32, (1, 128), 1)
    kept = (1.0 - inner_rate * decay_rate) ** steps
    adds_one, adds_two, terms, weights = [], [], [], []
    for step in range(steps):
        factor = jnp.sum(jnp.where(lane == step, factors, 0.0))
        shrunk_one = beta_one ** (step + 1)
        shrunk_two = beta_two ** (step + 1)
        left = (1.0 - inner_rate * decay_rate) ** (steps - 1 - step)
        adds_one.append(factor * ((1.0 - beta_one) / shrunk_one))
        adds_two.append(factor * factor * ((1.0 - beta_two) / shrunk_two))
        terms.append(epsilon / shrunk_two**0.5)
        weights.append(inner_rate * left * shrunk_one / shrunk_two**0.5)
    for at in range(0, length, 16):
        rows = slice(at, at + 16)
        delta = (1.0 - kept) * params_ref[rows, :]
        moment_one = one_ref[rows, :]
        moment_two = two_ref[rows, :]
        for step in range(steps):
            grad = grads_ref[step, rows, :].astype(jnp.float32)
            moment_one = moment_one + adds_one[step] * grad
            moment_two = moment_two + adds_two[step] * (grad * grad)
            root = moment_two * lax.rsqrt(moment_two) + terms[step]
            delta = delta + (weights[step] * moment_one) / root
        out_ref[rows, :] = delta.astype(out_ref.dtype)


def mean_kernel(in_ref, out_ref):
    replicas, length, _ = in_ref.shape
    for at in range(0, length, 16):
        rows = slice(at, at + 16)
        total = in_ref[0, rows, :].astype(jnp.float32)
        for group in range(1, replicas):
            total = total + in_ref[group, rows, :].astype(jnp.float32)
        total = (total / replicas).astype(out_ref.dtype)
        for group in range(replicas):
            out_ref[group, rows, :] = total


def outer_kernel(average_ref, params_ref, momentum_ref, new_params_ref, new_momentum_ref):
    _, length, _ = average_ref.shape
    for part, owner in enumerate(codes_order):
        slot = means_order.index(owner)
        for at in range(0, length, 16):
            rows = slice(part * length + at, part * length + at + 16)
            average = average_ref[slot, at : at + 16, :].astype(jnp.float32)
            momentum = outer_beta * momentum_ref[rows, :] + average
            new_momentum_ref[rows, :] = momentum
            new_params_ref[rows, :] = params_ref[rows, :] - outer_rate * (
                average + outer_beta * momentum
            )


def call(kernel, out_shape, *args, space=pltpu.VMEM, scratch=()):
    return pl.pallas_call(
        kernel,
        out_shape=out_shape,
        in_specs=[pl.BlockSpec(memory_space=space)] * len(args),
        scratch_shapes=scratch,
        compiler_params=pltpu.CompilerParams(vmem_limit_bytes=16 * 1024 * 1024),
    )(*args)


def body(outer_params, outer_momentum, first_moment, second_moment, inner_grads):
    replicas = lax.axis_size("group")
    shards = lax.axis_size("fsdp")
    rows, width = outer_params.shape
    length = rows * width // 128
    params = to_rows(outer_params)
    momentum = to_rows(outer_momentum)
    moment_one = to_rows(first_moment[0])
    moment_two = in_hbm(to_rows(second_moment[0]))
    grads = in_hbm(to_rows(inner_grads[0]))
    f32 = jnp.float32
    squares, grads, moment_two = call(
        squares_kernel,
        (
            jax.ShapeDtypeStruct((shards, 128), f32),
            jax.ShapeDtypeStruct(grads.shape, grads.dtype),
            jax.ShapeDtypeStruct(moment_two.shape, moment_two.dtype),
        ),
        grads,
        moment_two,
        space=pltpu.HBM,
        scratch=(pltpu.SemaphoreType.DMA((grads.shape[0],)), pltpu.SemaphoreType.DMA),
    )
    totals = lax.all_to_all(squares, "fsdp", 0, 0, tiled=True, axis_index_groups=[totals_order])
    delta = call(
        inner_kernel,
        jax.ShapeDtypeStruct((length, 128), sent),
        totals,
        params,
        moment_one,
        moment_two,
        grads,
    )
    delta = delta.reshape(replicas, length // replicas, 128)
    parts = lax.all_to_all(delta, "group", 0, 0, tiled=True, axis_index_groups=[codes_order])
    mean = call(mean_kernel, jax.ShapeDtypeStruct(parts.shape, sent), parts)
    average = lax.all_to_all(mean, "group", 0, 0, tiled=True, axis_index_groups=[means_order])
    out = jax.ShapeDtypeStruct((length, 128), f32)
    new_params, new_momentum = call(outer_kernel, (out, out), average, params, momentum)
    return (from_rows(new_params, rows, width), from_rows(new_momentum, rows, width))


def solution(mesh):
    return jax.shard_map(
        body,
        mesh=mesh,
        in_specs=(
            P("fsdp", None),
            P("fsdp", None),
            P("group", "fsdp", None),
            P("group", "fsdp", None),
            P("group", None, "fsdp", None),
        ),
        out_specs=(P("fsdp", None), P("fsdp", None)),
        check_vma=False,
    )
```
